32 devices in a mesh: grp: 2 (over y), slab: 4 (over z), row: 2 (over x), col: 2 (over core).
Axes of the slice: x: 2, y: 2, z: 4, core: 2. Of those that a mesh axis runs over, the one named last changes fastest.
Arguments:
- image: float32 [3, 64, 32, 256], P(None, ('grp', 'slab'), 'row', 'col'), parts along dimension 1, may hold values from -28 to 28, as said below
- brain_mask: int32 [64, 32, 256], P(('grp', 'slab'), 'row', 'col'), parts along dimension 0, may hold values from 0 to 1, as said below
- labels: int32 [64, 32, 256], P(('grp', 'slab'), 'row', 'col'), parts along dimension 0, may hold values from 0 to 7
Outputs:
- posterior: bfloat16 [8, 64, 32, 256], P(None, ('grp', 'slab'), 'row', 'col'), parts along dimension 1
- bias_field: float32 [3, 64, 32, 256], P(None, ('grp', 'slab'), 'row', 'col'), parts along dimension 1
- class_means: float32 [16, 3], P('grp'), parts along dimension 0
The draws below stay inside these ranges and needn't reach their ends.
There are 2 independent parts, one for each index of `grp`. The reference program is written for one: setup_inputs(seed, part) draws one part's arguments, and reference() takes and returns one part's arrays. A program takes and returns all parts, laid end to end along the dimension named above; each array names one. Nothing has to cross between parts.
Inputs may be any that keep to these rules, and one draw needn't show every extreme that they name: `image`: log intensities of 3 modalities. `brain_mask`: 1 marks a brain cell, 0 a cell outside.
All inputs are finite; a program needn't handle non-finite values.
Results may differ from the reference program's by a relative error of at most 0.001.
Values sent between devices are 32-bit elements; how exact they have to be, the bound alone decides.
A program may use at most 64 MiB of HBM per device.

```python
import math
import jax
import jax.numpy as jnp
from jax import lax

M = 3
K = 8
EM_ITERS = 2
MF_PASSES = 2
NS = 32
NR = 32
NC = 256


def class_draw(key):
    return jax.random.randint(jax.random.fold_in(key, 31), (NS, NR, NC), 0, K)


def draw_labels(key, part):
    return class_draw(key)


def draw_image(key, part):
    classes = class_draw(key)
    key_base = jax.random.fold_in(jax.random.fold_in(key, 11), 0)
    key_center = jax.random.fold_in(jax.random.fold_in(key, 11), 3)
    key_phase = jax.random.fold_in(jax.random.fold_in(key, 11), 4)
    extent = (M, NS, NR, NC)
    offsets = jnp.arange(M, dtype=jnp.float32).reshape(M, 1, 1, 1) * 0.5
    centers = jax.random.uniform(key_center, (K, M), jnp.float32, -2.0, 2.0)
    level = jnp.moveaxis(jnp.take(centers, classes, axis=0), 3, 0)
    phases = jax.random.uniform(key_phase, (M, 3), jnp.float32, -math.pi, math.pi)
    slab_pos = jnp.arange(NS, dtype=jnp.float32) / NS
    row_pos = jnp.arange(NR, dtype=jnp.float32) / NR
    col_pos = jnp.arange(NC, dtype=jnp.float32) / NC
    slab_wave = jnp.cos(2.0 * math.pi * slab_pos[None, :] + phases[:, 0:1])
    row_wave = jnp.cos(2.0 * math.pi * row_pos[None, :] + phases[:, 1:2])
    col_wave = jnp.cos(2.0 * math.pi * col_pos[None, :] + phases[:, 2:3])
    smooth = 0.7 * (slab_wave[:, :, None, None] + row_wave[:, None, :, None] + col_wave[:, None, None, :])
    return jnp.clip(jax.random.normal(key_base, extent, jnp.float32), -6.0, 6.0) + offsets + level + smooth


def draw_brain_mask(key, part):
    scores = jax.random.randint(jax.random.fold_in(key, 23), (NS, NR, NC), 0, 1000)
    levels = 250 + 650 * jnp.arange(NS, dtype=jnp.int32) // max(NS - 1, 1)
    return (scores < levels[:, None, None]).astype(jnp.int32)


def setup_inputs(seed: int = 0, part: int = 0) -> dict:
    splits = jax.random.split(jax.random.key(seed), 4)
    own_keys = jax.random.split(jax.random.fold_in(splits[3], part), 4)
    image = draw_image(jax.random.fold_in(jax.random.fold_in(splits[3], part), 71), part)
    brain_mask = draw_brain_mask(jax.random.fold_in(jax.random.fold_in(splits[3], part), 71), part)
    labels = draw_labels(jax.random.fold_in(jax.random.fold_in(splits[3], part), 71), part)
    return dict(image=image, brain_mask=brain_mask, labels=labels)


highest = lax.Precision.HIGHEST
coupling = 1.0
breadth = 8.0


def smooth_field(residual):
    spectrum = jnp.fft.fftn(residual, axes=(1, 2, 3))
    for axis_number, length in ((1, NS), (2, NR), (3, NC)):
        frequency = jnp.fft.fftfreq(length)
        response = jnp.exp(-2.0 * math.pi ** 2 * (length / breadth) ** 2 * frequency * frequency)
        target = [1, 1, 1, 1]
        target[axis_number] = length
        spectrum = spectrum * response.reshape(target)
    return jnp.real(jnp.fft.ifftn(spectrum, axes=(1, 2, 3))).astype(jnp.float32)


def neighbour_sum(belief):
    padded = jnp.pad(belief, ((0, 0), (1, 1), (1, 1), (1, 1)))
    total = padded[:, 2:, 1:-1, 1:-1] + padded[:, :-2, 1:-1, 1:-1]
    total = total + padded[:, 1:-1, 2:, 1:-1] + padded[:, 1:-1, :-2, 1:-1]
    total = total + padded[:, 1:-1, 1:-1, 2:] + padded[:, 1:-1, 1:-1, :-2]
    return total


def class_moments(belief, corrected):
    flat = belief.reshape(K, -1)
    values = corrected.reshape(M, -1)
    count = jnp.sum(flat, axis=1)
    first = jnp.dot(flat, values.T, precision=highest)
    means = first / (count + 1.0)[:, None]

    def one_class(inputs):
        weight, center = inputs
        offset = values - center[:, None]
        return jnp.sum(weight[None, :] * offset * offset, axis=1)

    spread = lax.map(one_class, (flat, means))
    variance = (spread + 1.0) / (count + 1.0)[:, None]
    return count, means, variance


def log_density(corrected, means, variance, prior):
    def one_class(inputs):
        center, scale, weight = inputs
        offset = corrected - center[:, None, None, None]
        terms = offset * offset / scale[:, None, None, None] + jnp.log(scale)[:, None, None, None]
        return jnp.log(weight) - 0.5 * jnp.sum(terms, axis=0)

    return lax.map(one_class, (means, variance, prior))


def reference(image, brain_mask, labels):
    inside = brain_mask.astype(jnp.float32)
    kinds = jnp.arange(K, dtype=jnp.int32)
    belief = (labels[None] == kinds[:, None, None, None]).astype(jnp.float32) * inside[None]
    bias_field = jnp.zeros_like(image)
    means = jnp.zeros((K, M), jnp.float32)
    for iteration in range(EM_ITERS):
        corrected = image - bias_field
        count, means, variance = class_moments(belief, corrected)
        prior = (count + 1.0) / (jnp.sum(count) + K)
        total = jnp.sum(belief, axis=0)
        removed = jnp.dot(means.T, belief.reshape(K, -1), precision=highest).reshape(image.shape)
        residual = image * total[None] - removed
        bias_field = smooth_field(residual)
        corrected = image - bias_field
        density = log_density(corrected, means, variance, prior)
        for sweep_index in range(MF_PASSES):
            belief = jax.nn.softmax(density + coupling * neighbour_sum(belief), axis=0) * inside[None]
    return belief.astype(jnp.bfloat16), bias_field, means
```

```python
import functools
import math

import jax
import jax.numpy as jnp
import numpy as np
from jax import lax
from jax.experimental import pallas as pl
from jax.experimental.pallas import tpu as pltpu
from jax.sharding import PartitionSpec as P

M = 3
K = 8
EM_ITERS = 2
MF_PASSES = 2
STEPS = EM_ITERS * MF_PASSES

MESH = pl.DeviceIdType.MESH
highest = lax.Precision.HIGHEST
coupling = 1.0
breadth = 8.0
f32 = jnp.float32


def response(length):
    folded = np.minimum(np.arange(length), length - np.arange(length)) / length
    return np.exp(-2.0 * np.pi**2 * (length / breadth) ** 2 * folded * folded)


def kernel_of(length):
    return np.real(np.fft.ifft(response(length)))


def column_tables(length):
    resp = response(length)
    kept = [j for j in range(length // 2 + 1) if np.float32(resp[j]) != 0]
    cells = np.arange(length)
    analysis, synthesis = [], []
    for j in kept:
        angle = 2.0 * np.pi * (j * cells % length) / length
        single = j == 0 or 2 * j == length
        weight = (1.0 if single else 2.0) * resp[j] / length
        analysis.append(np.cos(angle))
        synthesis.append(weight * np.cos(angle))
        if not single:
            analysis.append(np.sin(angle))
            synthesis.append(weight * np.sin(angle))
    rows = -(-len(analysis) // 8) * 8
    pad = np.zeros((rows - len(analysis), length))
    return np.concatenate([analysis, pad]), np.concatenate([synthesis, pad])


def row_matrix(nx, slabs, rows):
    line = kernel_of(nx * rows)
    at = np.arange(nx * rows)
    square = line[(at[None, :] - at[:, None]) % (nx * rows)].reshape(nx, rows, nx, rows)
    full = np.einsum("arbq,st->asrbtq", square, np.eye(slabs))
    size = nx * slabs * rows
    return full.reshape(size, size)


def slab_vectors(nz, slabs, rows):
    line = kernel_of(nz * slabs)
    out = np.zeros((nz, slabs, 1, slabs * rows))
    for dz in range(nz):
        for e in range(slabs):
            for s in range(slabs):
                value = line[(slabs * dz + s - (s - e) % slabs) % (nz * slabs)]
                out[dz, e, 0, s * rows : (s + 1) * rows] = value
    return out


def kernel(
    nz, nx, nc, chunk, owners,
    image, mask, labels, ana, syn, rowm, slabv,
    post, bias, means_out,
    bel, colh, cols, rowh, rows_s, corr, dens, res, mom, mom_s, mom_r, par,
    fwd_s, fwd_r, rolled, mixed, back_s, back_r,
    hs_sem, hr_sem, ms_sem, mr_sem, fs_sem, fr_sem, bs_sem, br_sem,
):
    _, S, R, C = image.shape
    count = nz * nx * nc
    z, x, c = lax.axis_index("slab"), lax.axis_index("row"), lax.axis_index("col")
    me = (z * nx + x) * nc + c
    J = ana.shape[1]

    def where_is(q):
        return {"slab": q // (nx * nc), "row": (q // nc) % nx, "col": q % nc}

    def peer(d):
        return lax.rem(me + d, count)

    def source(d):
        return lax.rem(me + count - d, count)

    lane = lax.broadcasted_iota(jnp.int32, (R, C), 1)
    lane3 = lax.broadcasted_iota(jnp.int32, (K, R, C), 2)
    sub3 = lax.broadcasted_iota(jnp.int32, (K, R, C), 1)

    for v in range(STEPS):
        bel[v, :, 0] = jnp.zeros((K, R, C), f32)
        bel[v, :, S + 1] = jnp.zeros((K, R, C), f32)
    rowh[...] = jnp.zeros(rowh.shape, f32)

    barrier = pltpu.get_barrier_semaphore()

    def greet(d, carry):
        pl.semaphore_signal(barrier, inc=1, device_id=where_is(peer(d)), device_id_type=MESH)
        return carry

    lax.fori_loop(1, count, greet, 0)

    def halo_copies(v):
        copies = [
            (z < nz - 1, z > 0, bel.at[v, :, S], bel.at[v, :, 0], {"slab": z + 1}, 0),
            (z > 0, z < nz - 1, bel.at[v, :, 1], bel.at[v, :, S + 1], {"slab": z - 1}, 1),
            (x < nx - 1, x > 0, rows_s.at[v, 1], rowh.at[v, 0], {"row": x + 1}, 2),
            (x > 0, x < nx - 1, rows_s.at[v, 0], rowh.at[v, 1], {"row": x - 1}, 3),
        ]
        if nc == 2:
            copies.append((None, None, cols.at[v], colh.at[v], {"col": 1 - c}, 4))
        out = []
        for sends, receives, src, dst, device, n in copies:
            copy = pltpu.make_async_remote_copy(
                src_ref=src, dst_ref=dst, send_sem=hs_sem.at[v, n], recv_sem=hr_sem.at[v, n],
                device_id=device, device_id_type=MESH,
            )
            out.append((sends, receives, copy))
        return out

    def under(condition, action):
        if condition is None:
            action()
        else:
            pl.when(condition)(action)

    def halo_start(v):
        for sends, _, copy in halo_copies(v):
            under(sends, copy.start)

    def halo_wait(v):
        for _, receives, copy in halo_copies(v):
            under(receives, copy.wait_recv)

    def halo_drain(v):
        for sends, _, copy in halo_copies(v):
            under(sends, copy.wait_send)

    def keep(v, s, block):
        bel[v, :, s + 1] = block
        rows_s[v, 0, s] = block[:, 0]
        rows_s[v, 1, s] = block[:, R - 1]
        if nc == 2:
            packed = jnp.zeros((R, C), f32)
            for k in range(K):
                last = jnp.broadcast_to(block[k, :, C - 1 : C], (R, C))
                first = jnp.broadcast_to(block[k, :, 0:1], (R, C))
                packed = jnp.where(lane == k, jnp.where(c == 0, last, first), packed)
            cols[v, s] = packed

    def begin(s, carry):
        seen = labels[s]
        inside = mask[s].astype(f32)
        block = jnp.stack([jnp.where(seen == k, inside, 0.0) for k in range(K)])
        keep(0, s, block)
        return carry

    lax.fori_loop(0, S, begin, 0)
    pl.semaphore_wait(barrier, count - 1)
    halo_start(0)
    mom[...] = jnp.zeros(mom.shape, f32)

    def exchange_copy(kind, it, d, target, owner):
        if kind == 0:
            src, dst, ss, rs = mom_s.at[it], mom_r.at[it, owner], ms_sem, mr_sem
        elif kind == 1:
            src, dst, ss, rs = fwd_s.at[it, target], fwd_r.at[it, owner], fs_sem, fr_sem
        else:
            src, dst, ss, rs = back_s.at[it, target // nc], back_r.at[it, owner], bs_sem, br_sem
        return pltpu.make_async_remote_copy(
            src_ref=src, dst_ref=dst, send_sem=ss.at[it, d], recv_sem=rs.at[it, d],
            device_id=where_is(target), device_id_type=MESH,
        )

    def each(action):
        def body(d, carry):
            action(d)
            return carry

        lax.fori_loop(1, count, body, 0)

    def moments_out(it):
        for k in range(K):
            weight = bel[it * MF_PASSES, k, 1 : S + 1]
            total = jnp.sum(jnp.sum(weight, axis=0), axis=0, keepdims=True)
            for m in range(M):
                value = corr[m] if it else image[m]
                first = weight * value
                second = first * value
                mom[m * K + k : m * K + k + 1] = total
                at = (M + m) * K + k
                mom[at : at + 1] = jnp.sum(jnp.sum(first, axis=0), axis=0, keepdims=True)
                at = (2 * M + m) * K + k
                mom[at : at + 1] = jnp.sum(jnp.sum(second, axis=0), axis=0, keepdims=True)
        sums = lax.dot_general(
            jnp.ones((8, C), f32), mom[...], (((1,), (1,)), ((), ())),
            precision=highest, preferred_element_type=f32,
        )
        mom_s[it] = sums[0:1]
        each(lambda d: exchange_copy(0, it, d, peer(d), me).start())
        mom_r[it, me] = sums[0:1]

    def moments_in(it):
        each(lambda d: exchange_copy(0, it, d, me, source(d)).wait_recv())
        sums = jnp.broadcast_to(jnp.sum(mom_r[it], axis=0), (8, 128))
        width = M * K
        lanes = lax.broadcasted_iota(jnp.int32, (8, 128), 1)
        counts = sums
        first = pltpu.roll(sums, 128 - width, 1)
        second = pltpu.roll(sums, 128 - 2 * width, 1)
        scale = 1.0 / (counts + 1.0)
        means = first * scale
        spread = second - 2.0 * means * first + means * means * counts
        variance = jnp.where(lanes < width, (spread + 1.0) * scale, 1.0)
        half = 0.5 / variance
        logs = jnp.log(variance)
        everything = jnp.sum(jnp.where(lanes < K, counts, 0.0), axis=1, keepdims=True)
        prior = jnp.where(lanes < K, (counts + 1.0) / (everything + K), 1.0)
        logs_sum = logs
        for m in range(1, M):
            logs_sum = logs_sum + pltpu.roll(logs, 128 - m * K, 1)
        base = jnp.log(prior) - 0.5 * logs_sum
        for n in range(width):
            par[n] = jnp.broadcast_to(means[:, n : n + 1], (8, 128))
            par[width + n] = jnp.broadcast_to(half[:, n : n + 1], (8, 128))
        for k in range(K):
            par[2 * width + k] = jnp.broadcast_to(base[:, k : k + 1], (8, 128))
        if it == EM_ITERS - 1:
            rows = lax.broadcasted_iota(jnp.int32, (8, 128), 0)
            table = jnp.zeros((8, 128), f32)
            for k in range(K):
                for m in range(M):
                    table = jnp.where((rows == k) & (lanes == m), par[m * K + k], table)
            means_out[...] = table[:K, :M]

    def param(n):
        one = par[n, 0:1]
        return jnp.broadcast_to(one, (R, C))

    def residual(it):
        v = it * MF_PASSES

        def body(s, carry):
            block = bel[v, :, s + 1]
            total = jnp.sum(block, axis=0)
            for m in range(M):
                value = image[m, s] * total
                for k in range(K):
                    value = value - block[k] * param(m * K + k)
                res[m, s] = value
            return carry

        lax.fori_loop(0, S, body, 0)

    def smooth(it):
        table = ana[c]
        coefs = [
            lax.dot_general(
                table, res[m].reshape(S * R, C), (((1,), (1,)), ((), ())),
                precision=highest, preferred_element_type=f32,
            )
            for m in range(M)
        ]
        tall = jnp.concatenate(coefs, axis=0)
        spare = owners * chunk - M * J
        if spare:
            tall = jnp.concatenate([tall, jnp.zeros((spare, S * R), f32)], axis=0)
        fwd_s[it] = tall.reshape(owners, chunk, S * R)

        def send(d):
            @pl.when(peer(d) < owners)
            def _():
                exchange_copy(1, it, d, peer(d), me).start()

        each(send)

        @pl.when(me < owners)
        def _():
            fwd_r[it, me] = fwd_s[it, me]
            each(lambda d: exchange_copy(1, it, d, me, source(d)).wait_recv())
            stack = []
            for zz in range(nz):
                across = []
                for xx in range(nx):
                    at = (zz * nx + xx) * nc
                    tile = fwd_r[it, at]
                    for cc in range(1, nc):
                        tile = tile + fwd_r[it, at + cc]
                    across.append(tile)
                stack.append(jnp.concatenate(across, axis=1))
            mixed[...] = jnp.dot(
                jnp.concatenate(stack, axis=0), rowm[...],
                precision=highest, preferred_element_type=f32,
            )
            for xx in range(nx):
                for zz in range(nz):
                    tile = mixed[zz * chunk : (zz + 1) * chunk, xx * S * R : (xx + 1) * S * R]
                    for e in range(S):
                        rolled[zz, e] = pltpu.roll(tile, e * R, 1) if e else tile

                def body(zq, carry):
                    total = jnp.zeros((chunk, S * R), f32)
                    for zz in range(nz):
                        dz = lax.rem(zq + nz - zz, nz)
                        for e in range(S):
                            total = total + rolled[zz, e] * slabv[dz, e]
                    back_s[it, zq * nx + xx] = total
                    return carry

                lax.fori_loop(0, nz, body, 0)
            each(lambda d: exchange_copy(2, it, d, peer(d), me).start())
            back_r[it, me] = back_s[it, me // nc]

        def wait(d):
            @pl.when(source(d) < owners)
            def _():
                exchange_copy(2, it, d, me, source(d)).wait_recv()

        each(wait)
        flat = back_r[it].reshape(owners * chunk, S * R)
        table = syn[c]
        for m in range(M):
            field = lax.dot_general(
                flat[m * J : (m + 1) * J], table, (((0,), (0,)), ((), ())),
                precision=highest, preferred_element_type=f32,
            ).reshape(S, R, C)
            if it == EM_ITERS - 1:
                bias[m] = field
            corr[m] = image[m] - field

    def density():
        width = M * K

        def body(s, carry):
            for k in range(K):
                value = param(2 * width + k)
                for m in range(M):
                    offset = corr[m, s] - param(m * K + k)
                    value = value - offset * offset * param(width + m * K + k)
                dens[k, s] = value
            return carry

        lax.fori_loop(0, S, body, 0)

    def sweep(v):
        edge = jnp.where(c == 0, C - 1, 0)

        def body(s, carry):
            block = bel[v, :, s + 1]
            total = bel[v, :, s] + bel[v, :, s + 2]
            total = total + jnp.where(sub3 == 0, rowh[v, 0, s][:, None, :], pltpu.roll(block, 1, 1))
            total = total + jnp.where(
                sub3 == R - 1, rowh[v, 1, s][:, None, :], pltpu.roll(block, R - 1, 1)
            )
            if nc == 2:
                packed = colh[v, s]
                beyond = jnp.stack(
                    [jnp.broadcast_to(packed[:, k : k + 1], (R, C)) for k in range(K)]
                )
                total = total + jnp.where(lane3 == edge, beyond, 0.0)
            total = total + jnp.where(lane3 == 0, 0.0, pltpu.roll(block, 1, 2))
            total = total + jnp.where(lane3 == C - 1, 0.0, pltpu.roll(block, C - 1, 2))
            logits = dens[:, s] + coupling * total
            powers = jnp.exp(logits - jnp.max(logits, axis=0, keepdims=True))
            scale = mask[s].astype(f32) / jnp.sum(powers, axis=0)
            fresh = powers * scale[None]
            if v == STEPS - 1:
                post[:, s] = fresh.astype(post.dtype)
            else:
                keep(v + 1, s, fresh)
            return carry

        lax.fori_loop(0, S, body, 0)

    for it in range(EM_ITERS):
        moments_out(it)
        moments_in(it)
        residual(it)
        smooth(it)
        density()
        for p in range(MF_PASSES):
            v = it * MF_PASSES + p
            halo_wait(v)
            sweep(v)
            if v < STEPS - 1:
                halo_start(v + 1)

    for v in range(STEPS):
        halo_drain(v)
    for it in range(EM_ITERS):
        def drain(d):
            exchange_copy(0, it, d, peer(d), me).wait_send()

            @pl.when(peer(d) < owners)
            def _():
                exchange_copy(1, it, d, peer(d), me).wait_send()

            @pl.when(me < owners)
            def _():
                exchange_copy(2, it, d, peer(d), me).wait_send()

        each(drain)


def local(nz, nx, nc, image, brain_mask, labels):
    _, S, R, C = image.shape
    count = nz * nx * nc
    analysis, synthesis = column_tables(C * nc)
    J = analysis.shape[0]
    tiles = M * J // 8
    chunk = 8 * -(-tiles // count)
    owners = -(-M * J // chunk)
    ana = jnp.asarray(analysis.reshape(J, nc, C).transpose(1, 0, 2), f32)
    syn = jnp.asarray(synthesis.reshape(J, nc, C).transpose(1, 0, 2), f32)
    rowm = jnp.asarray(row_matrix(nx, S, R), f32)
    slabv = jnp.asarray(slab_vectors(nz, S, R), f32)
    vmem = pl.BlockSpec(memory_space=pltpu.VMEM)
    lanes = S * R
    return pl.pallas_call(
        functools.partial(kernel, nz, nx, nc, chunk, owners),
        out_shape=(
            jax.ShapeDtypeStruct((K, S, R, C), jnp.bfloat16),
            jax.ShapeDtypeStruct((M, S, R, C), f32),
            jax.ShapeDtypeStruct((K, M), f32),
        ),
        in_specs=[vmem] * 7,
        out_specs=(vmem, vmem, vmem),
        scratch_shapes=[
            pltpu.VMEM((STEPS, K, S + 2, R, C), f32),
            pltpu.VMEM((STEPS, S, R, C), f32),
            pltpu.VMEM((STEPS, S, R, C), f32),
            pltpu.VMEM((STEPS, 2, S, K, C), f32),
            pltpu.VMEM((STEPS, 2, S, K, C), f32),
            pltpu.VMEM((M, S, R, C), f32),
            pltpu.VMEM((K, S, R, C), f32),
            pltpu.VMEM((M, S, R, C), f32),
            pltpu.VMEM((128, C), f32),
            pltpu.VMEM((EM_ITERS, 1, 128), f32),
            pltpu.VMEM((EM_ITERS, count, 1, 128), f32),
            pltpu.VMEM((2 * M * K + K, 8, 128), f32),
            pltpu.VMEM((EM_ITERS, owners, chunk, lanes), f32),
            pltpu.VMEM((EM_ITERS, count, chunk, lanes), f32),
            pltpu.VMEM((nz, S, chunk, lanes), f32),
            pltpu.VMEM((nz * chunk, nx * lanes), f32),
            pltpu.VMEM((EM_ITERS, nz * nx, chunk, lanes), f32),
            pltpu.VMEM((EM_ITERS, owners, chunk, lanes), f32),
            pltpu.SemaphoreType.DMA((STEPS, 5)),
            pltpu.SemaphoreType.DMA((STEPS, 5)),
        ]
        + [pltpu.SemaphoreType.DMA((EM_ITERS, count))] * 6,
        compiler_params=pltpu.CompilerParams(
            collective_id=0, has_side_effects=True, vmem_limit_bytes=48 * 1024 * 1024
        ),
    )(image, brain_mask, labels, ana, syn, rowm, slabv)


def solution(mesh):
    placed = (
        P(None, ("grp", "slab"), "row", "col"),
        P(("grp", "slab"), "row", "col"),
        P(("grp", "slab"), "row", "col"),
    )
    return jax.shard_map(
        functools.partial(local, mesh.shape["slab"], mesh.shape["row"], mesh.shape["col"]),
        mesh=mesh,
        in_specs=placed,
        out_specs=(
            P(None, ("grp", "slab"), "row", "col"),
            P(None, ("grp", "slab"), "row", "col"),
            P("grp", None),
        ),
        check_vma=False,
    )
```

```python
import functools
import math

import jax
import jax.numpy as jnp
import numpy as np
from jax import lax
from jax.experimental import pallas as pl
from jax.experimental.pallas import tpu as pltpu
from jax.sharding import PartitionSpec as P

M = 3
K = 8
EM_ITERS = 2
MF_PASSES = 2
STEPS = EM_ITERS * MF_PASSES

MESH = pl.DeviceIdType.MESH
highest = lax.Precision.HIGHEST
coupling = 1.0
breadth = 8.0
f32 = jnp.float32


def response(length):
    folded = np.minimum(np.arange(length), length - np.arange(length)) / length
    return np.exp(-2.0 * np.pi**2 * (length / breadth) ** 2 * folded * folded)


def kernel_of(length):
    return np.real(np.fft.ifft(response(length)))


def column_tables(length):
    resp = response(length)
    kept = [j for j in range(length // 2 + 1) if np.float32(resp[j]) != 0]
    cells = np.arange(length)
    analysis, synthesis = [], []
    for j in kept:
        angle = 2.0 * np.pi * (j * cells % length) / length
        single = j == 0 or 2 * j == length
        weight = (1.0 if single else 2.0) * resp[j] / length
        analysis.append(np.cos(angle))
        synthesis.append(weight * np.cos(angle))
        if not single:
            analysis.append(np.sin(angle))
            synthesis.append(weight * np.sin(angle))
    rows = -(-len(analysis) // 8) * 8
    pad = np.zeros((rows - len(analysis), length))
    return np.concatenate([analysis, pad]), np.concatenate([synthesis, pad])


def row_matrix(nx, slabs, rows):
    line = kernel_of(nx * rows)
    at = np.arange(nx * rows)
    square = line[(at[None, :] - at[:, None]) % (nx * rows)].reshape(nx, rows, nx, rows)
    full = np.einsum("arbq,st->asrbtq", square, np.eye(slabs))
    size = nx * slabs * rows
    return full.reshape(size, size)


def slab_vectors(nz, slabs, rows):
    line = kernel_of(nz * slabs)
    out = np.zeros((nz, slabs, 1, slabs * rows))
    for dz in range(nz):
        for e in range(slabs):
            for s in range(slabs):
                value = line[(slabs * dz + s - (s - e) % slabs) % (nz * slabs)]
                out[dz, e, 0, s * rows : (s + 1) * rows] = value
    return out


def kernel(
    nz, nx, nc, chunk, owners,
    image_h, mask_h, labels_h, ana_h, syn_h, rowm_h, slabv_h,
    post, bias, means_out,
    image, mask, labels, ana, syn, rowm, slabv,
    bel, colh, cols, rowh, rows_s, corr, dens, res, mom, mom_s, mom_r, par,
    fwd_s, fwd_r, rolled, mixed, back_s, back_r,
    hs_sem, hr_sem, ms_sem, mr_sem, fs_sem, fr_sem, bs_sem, br_sem, in_sem,
):
    _, S, R, C = image.shape
    count = nz * nx * nc
    z, x, c = lax.axis_index("slab"), lax.axis_index("row"), lax.axis_index("col")
    me = (z * nx + x) * nc + c
    J = ana.shape[0]
    everyone = owners == count

    fetches = [
        pltpu.make_async_copy(src, dst, in_sem.at[n])
        for n, (src, dst) in enumerate(
            [
                (labels_h, labels), (mask_h, mask), (image_h, image), (ana_h.at[c], ana),
                (rowm_h, rowm), (slabv_h, slabv), (syn_h.at[c], syn),
            ]
        )
    ]
    for fetch in fetches:
        fetch.start()

    def moved(at, by, size):
        if size == 1:
            return at
        there = at + by
        return jnp.where(there >= size, there - size, there)

    def shifted(dz, dx, dc):
        zz, xx, cc = moved(z, dz, nz), moved(x, dx, nx), moved(c, dc, nc)
        return {"slab": zz, "row": xx, "col": cc}, (zz * nx + xx) * nc + cc

    def each(action):
        if count <= 32:
            for d in range(count - 1, 0, -1):
                action(*shifted(d // (nx * nc), d // nc % nx, d % nc))
        else:
            def body(d, carry):
                action(*shifted(d // (nx * nc), d // nc % nx, d % nc))
                return carry

            lax.fori_loop(1, count, body, 0)

    lane = lax.broadcasted_iota(jnp.int32, (R, C), 1)
    lane3 = lax.broadcasted_iota(jnp.int32, (K, R, C), 2)
    sub3 = lax.broadcasted_iota(jnp.int32, (K, R, C), 1)

    for v in range(STEPS):
        bel[v, :, 0] = jnp.zeros((K, R, C), f32)
        bel[v, :, S + 1] = jnp.zeros((K, R, C), f32)
    rowh[...] = jnp.zeros(rowh.shape, f32)

    barrier = pltpu.get_barrier_semaphore()

    each(
        lambda device, q: pl.semaphore_signal(
            barrier, inc=1, device_id=device, device_id_type=MESH
        )
    )

    def halo_copies(v):
        copies = [
            (z < nz - 1, z > 0, bel.at[v, :, S], bel.at[v, :, 0], {"slab": z + 1}, 0),
            (z > 0, z < nz - 1, bel.at[v, :, 1], bel.at[v, :, S + 1], {"slab": z - 1}, 1),
            (x < nx - 1, x > 0, rows_s.at[v, 1], rowh.at[v, 0], {"row": x + 1}, 2),
            (x > 0, x < nx - 1, rows_s.at[v, 0], rowh.at[v, 1], {"row": x - 1}, 3),
        ]
        if nc == 2:
            copies.append((None, None, cols.at[v], colh.at[v], {"col": 1 - c}, 4))
        out = []
        for sends, receives, src, dst, device, n in copies:
            copy = pltpu.make_async_remote_copy(
                src_ref=src, dst_ref=dst, send_sem=hs_sem.at[v, n], recv_sem=hr_sem.at[v, n],
                device_id=device, device_id_type=MESH,
            )
            out.append((sends, receives, copy))
        return out

    def under(condition, action):
        if condition is None:
            action()
        else:
            pl.when(condition)(action)

    def halo_start(v, first=0, last=5):
        for sends, _, copy in halo_copies(v)[first:last]:
            under(sends, copy.start)

    def halo_wait(v):
        for _, receives, copy in halo_copies(v):
            under(receives, copy.wait_recv)

    def halo_drain(v):
        for sends, _, copy in halo_copies(v):
            under(sends, copy.wait_send)

    def keep(v, s, block):
        bel[v, :, s + 1] = block
        rows_s[v, 0, s] = block[:, 0]
        rows_s[v, 1, s] = block[:, R - 1]
        if nc == 2:
            packed = jnp.zeros((R, C), f32)
            for k in range(K):
                last = jnp.broadcast_to(block[k, :, C - 1 : C], (R, C))
                first = jnp.broadcast_to(block[k, :, 0:1], (R, C))
                packed = jnp.where(lane == k, jnp.where(c == 0, last, first), packed)
            cols[v, s] = packed

    def begin(s, carry):
        seen = labels[s]
        inside = mask[s].astype(f32)
        block = jnp.stack([jnp.where(seen == k, inside, 0.0) for k in range(K)])
        keep(0, s, block)
        return carry

    fetches[0].wait()
    fetches[1].wait()
    lax.fori_loop(0, S, begin, 0)
    mom[...] = jnp.zeros(mom.shape, f32)
    fetches[2].wait()

    def send(src, dst, send_sem, recv_sem, device):
        pltpu.make_async_remote_copy(
            src_ref=src, dst_ref=dst, send_sem=send_sem, recv_sem=recv_sem,
            device_id=device, device_id_type=MESH,
        ).start()

    def await_bytes(buffer, n, sem):
        whole = buffer.at[pl.ds(0, n)]
        pltpu.make_async_copy(whole, whole, sem).wait()

    def moments_out(it):
        for k in range(K):
            weight = bel[it * MF_PASSES, k, 1 : S + 1]
            total = jnp.sum(jnp.sum(weight, axis=0), axis=0, keepdims=True)
            for m in range(M):
                value = corr[m] if it else image[m]
                first = weight * value
                second = first * value
                mom[m * K + k : m * K + k + 1] = total
                at = (M + m) * K + k
                mom[at : at + 1] = jnp.sum(jnp.sum(first, axis=0), axis=0, keepdims=True)
                at = (2 * M + m) * K + k
                mom[at : at + 1] = jnp.sum(jnp.sum(second, axis=0), axis=0, keepdims=True)
        sums = lax.dot_general(
            jnp.ones((8, C), f32), mom[...], (((1,), (1,)), ((), ())),
            precision=highest, preferred_element_type=f32,
        )
        mom_s[it] = sums[0:1]
        if it == 0:
            pl.semaphore_wait(barrier, count - 1)
        each(
            lambda device, q: send(
                mom_s.at[it], mom_r.at[it, me], ms_sem.at[it], mr_sem.at[it], device
            )
        )
        halo_start(it * MF_PASSES)
        mom_r[it, me] = sums[0:1]

    def moments_in(it):
        await_bytes(mom_r.at[it], count - 1, mr_sem.at[it])
        sums = jnp.broadcast_to(jnp.sum(mom_r[it], axis=0), (8, 128))
        width = M * K
        lanes = lax.broadcasted_iota(jnp.int32, (8, 128), 1)
        counts = sums
        first = pltpu.roll(sums, 128 - width, 1)
        second = pltpu.roll(sums, 128 - 2 * width, 1)
        scale = 1.0 / (counts + 1.0)
        means = first * scale
        spread = second - 2.0 * means * first + means * means * counts
        variance = jnp.where(lanes < width, (spread + 1.0) * scale, 1.0)
        half = 0.5 / variance
        logs = jnp.log(variance)
        everything = jnp.sum(jnp.where(lanes < K, counts, 0.0), axis=1, keepdims=True)
        prior = jnp.where(lanes < K, (counts + 1.0) / (everything + K), 1.0)
        logs_sum = logs
        for m in range(1, M):
            logs_sum = logs_sum + pltpu.roll(logs, 128 - m * K, 1)
        base = jnp.log(prior) - 0.5 * logs_sum
        for n in range(width):
            par[n] = jnp.broadcast_to(means[:, n : n + 1], (8, 128))
            par[width + n] = jnp.broadcast_to(half[:, n : n + 1], (8, 128))
        for k in range(K):
            par[2 * width + k] = jnp.broadcast_to(base[:, k : k + 1], (8, 128))
        if it == EM_ITERS - 1:
            rows = lax.broadcasted_iota(jnp.int32, (8, 128), 0)
            table = jnp.zeros((8, 128), f32)
            for k in range(K):
                for m in range(M):
                    table = jnp.where((rows == k) & (lanes == m), par[m * K + k], table)
            means_out[...] = table[:K, :M]

    def param(n):
        one = par[n, 0:1]
        return jnp.broadcast_to(one, (R, C))

    def residual(it):
        v = it * MF_PASSES

        def body(s, carry):
            block = bel[v, :, s + 1]
            total = jnp.sum(block, axis=0)
            for m in range(M):
                value = image[m, s] * total
                for k in range(K):
                    value = value - block[k] * param(m * K + k)
                res[m, s] = value
            return carry

        lax.fori_loop(0, S, body, 0)

    def smooth(it):
        if it == 0:
            fetches[3].wait()
        table = ana[...]
        coefs = [
            lax.dot_general(
                table, res[m].reshape(S * R, C), (((1,), (1,)), ((), ())),
                precision=highest, preferred_element_type=f32,
            )
            for m in range(M)
        ]
        tall = jnp.concatenate(coefs, axis=0)
        spare = owners * chunk - M * J
        if spare:
            tall = jnp.concatenate([tall, jnp.zeros((spare, S * R), f32)], axis=0)
        fwd_s[it] = tall.reshape(owners, chunk, S * R)

        def forward(device, q):
            def go():
                send(fwd_s.at[it, q], fwd_r.at[it, me], fs_sem.at[it], fr_sem.at[it], device)

            under(None if everyone else q < owners, go)

        each(forward)
        if it == 0:
            fetches[4].wait()
            fetches[5].wait()

        def own():
            fwd_r[it, me] = fwd_s[it, me]
            await_bytes(fwd_r.at[it], count - 1, fr_sem.at[it])
            stack = []
            for zz in range(nz):
                across = []
                for xx in range(nx):
                    at = (zz * nx + xx) * nc
                    tile = fwd_r[it, at]
                    for cc in range(1, nc):
                        tile = tile + fwd_r[it, at + cc]
                    across.append(tile)
                stack.append(jnp.concatenate(across, axis=1))
            mixed[...] = jnp.dot(
                jnp.concatenate(stack, axis=0), rowm[...],
                precision=highest, preferred_element_type=f32,
            )
            for xx in range(nx):
                for zz in range(nz):
                    tile = mixed[zz * chunk : (zz + 1) * chunk, xx * S * R : (xx + 1) * S * R]
                    for e in range(S):
                        rolled[zz, e] = pltpu.roll(tile, e * R, 1) if e else tile

                def body(zq, carry):
                    total = jnp.zeros((chunk, S * R), f32)
                    for zz in range(nz):
                        dz = lax.rem(zq + nz - zz, nz)
                        for e in range(S):
                            total = total + rolled[zz, e] * slabv[dz, e]
                    back_s[it, zq * nx + xx] = total
                    return carry

                lax.fori_loop(0, nz, body, 0)
            each(
                lambda device, q: send(
                    back_s.at[it, q // nc], back_r.at[it, me], bs_sem.at[it], br_sem.at[it], device
                )
            )
            back_r[it, me] = back_s[it, me // nc]

        under(None if everyone else me < owners, own)
        if it == 0:
            fetches[6].wait()
        if everyone:
            await_bytes(back_r.at[it], owners - 1, br_sem.at[it])
        else:
            under(me < owners, lambda: await_bytes(back_r.at[it], owners - 1, br_sem.at[it]))
            under(me >= owners, lambda: await_bytes(back_r.at[it], owners, br_sem.at[it]))
        flat = back_r[it].reshape(owners * chunk, S * R)
        table = syn[...]
        for m in range(M):
            field = lax.dot_general(
                flat[m * J : (m + 1) * J], table, (((0,), (0,)), ((), ())),
                precision=highest, preferred_element_type=f32,
            ).reshape(S, R, C)
            if it == EM_ITERS - 1:
                bias[m] = field
            corr[m] = image[m] - field

    def density():
        width = M * K

        def body(s, carry):
            for k in range(K):
                value = param(2 * width + k)
                for m in range(M):
                    offset = corr[m, s] - param(m * K + k)
                    value = value - offset * offset * param(width + m * K + k)
                dens[k, s] = value
            return carry

        lax.fori_loop(0, S, body, 0)

    def sweep(v):
        edge = jnp.where(c == 0, C - 1, 0)

        def body(s, carry):
            block = bel[v, :, s + 1]
            total = bel[v, :, s] + bel[v, :, s + 2]
            total = total + jnp.where(sub3 == 0, rowh[v, 0, s][:, None, :], pltpu.roll(block, 1, 1))
            total = total + jnp.where(
                sub3 == R - 1, rowh[v, 1, s][:, None, :], pltpu.roll(block, R - 1, 1)
            )
            if nc == 2:
                packed = colh[v, s]
                beyond = jnp.stack(
                    [jnp.broadcast_to(packed[:, k : k + 1], (R, C)) for k in range(K)]
                )
                total = total + jnp.where(lane3 == edge, beyond, 0.0)
            total = total + jnp.where(lane3 == 0, 0.0, pltpu.roll(block, 1, 2))
            total = total + jnp.where(lane3 == C - 1, 0.0, pltpu.roll(block, C - 1, 2))
            logits = dens[:, s] + coupling * total
            powers = jnp.exp(logits - jnp.max(logits, axis=0, keepdims=True))
            scale = mask[s].astype(f32) / jnp.sum(powers, axis=0)
            fresh = powers * scale[None]
            if v == STEPS - 1:
                post[:, s] = fresh.astype(post.dtype)
            else:
                keep(v + 1, s, fresh)
            return carry

        lax.fori_loop(0, 2, lambda i, carry: body(i * (S - 1), carry), 0)
        if v % MF_PASSES < MF_PASSES - 1:
            halo_start(v + 1, 0, 2)
        lax.fori_loop(1, S - 1, body, 0)
        if v % MF_PASSES < MF_PASSES - 1:
            halo_start(v + 1, 2, 5)

    for it in range(EM_ITERS):
        moments_out(it)
        moments_in(it)
        residual(it)
        smooth(it)
        density()
        for p in range(MF_PASSES):
            v = it * MF_PASSES + p
            halo_wait(v)
            sweep(v)

    for v in range(STEPS):
        halo_drain(v)
    for it in range(EM_ITERS):
        await_bytes(mom_r.at[it], count - 1, ms_sem.at[it])
        if everyone:
            await_bytes(fwd_r.at[it], owners - 1, fs_sem.at[it])
            await_bytes(fwd_r.at[it], count - 1, bs_sem.at[it])
        else:
            under(me >= owners, lambda: await_bytes(fwd_r.at[it], owners, fs_sem.at[it]))

            def drain():
                if owners > 1:
                    await_bytes(fwd_r.at[it], owners - 1, fs_sem.at[it])
                await_bytes(fwd_r.at[it], count - 1, bs_sem.at[it])

            under(me < owners, drain)


def local(nz, nx, nc, image, brain_mask, labels):
    _, S, R, C = image.shape
    count = nz * nx * nc
    analysis, synthesis = column_tables(C * nc)
    J = analysis.shape[0]
    tiles = M * J // 8
    chunk = 8 * -(-tiles // count)
    owners = -(-M * J // chunk)
    if count <= 2 * owners:
        owners = count
    ana = jnp.asarray(analysis.reshape(J, nc, C).transpose(1, 0, 2), f32)
    syn = jnp.asarray(synthesis.reshape(J, nc, C).transpose(1, 0, 2), f32)
    rowm = jnp.asarray(row_matrix(nx, S, R), f32)
    slabv = jnp.asarray(slab_vectors(nz, S, R), f32)
    vmem = pl.BlockSpec(memory_space=pltpu.VMEM)
    lanes = S * R
    return pl.pallas_call(
        functools.partial(kernel, nz, nx, nc, chunk, owners),
        out_shape=(
            jax.ShapeDtypeStruct((K, S, R, C), jnp.bfloat16),
            jax.ShapeDtypeStruct((M, S, R, C), f32),
            jax.ShapeDtypeStruct((K, M), f32),
        ),
        in_specs=[pl.BlockSpec(memory_space=pl.ANY)] * 7,
        out_specs=(vmem, vmem, vmem),
        scratch_shapes=[
            pltpu.VMEM((M, S, R, C), f32),
            pltpu.VMEM((S, R, C), jnp.int32),
            pltpu.VMEM((S, R, C), jnp.int32),
            pltpu.VMEM((J, C), f32),
            pltpu.VMEM((J, C), f32),
            pltpu.VMEM(rowm.shape, f32),
            pltpu.VMEM(slabv.shape, f32),
            pltpu.VMEM((STEPS, K, S + 2, R, C), f32),
            pltpu.VMEM((STEPS, S, R, C), f32),
            pltpu.VMEM((STEPS, S, R, C), f32),
            pltpu.VMEM((STEPS, 2, S, K, C), f32),
            pltpu.VMEM((STEPS, 2, S, K, C), f32),
            pltpu.VMEM((M, S, R, C), f32),
            pltpu.VMEM((K, S, R, C), f32),
            pltpu.VMEM((M, S, R, C), f32),
            pltpu.VMEM((128, C), f32),
            pltpu.VMEM((EM_ITERS, 1, 128), f32),
            pltpu.VMEM((EM_ITERS, count, 1, 128), f32),
            pltpu.VMEM((2 * M * K + K, 8, 128), f32),
            pltpu.VMEM((EM_ITERS, owners, chunk, lanes), f32),
            pltpu.VMEM((EM_ITERS, count, chunk, lanes), f32),
            pltpu.VMEM((nz, S, chunk, lanes), f32),
            pltpu.VMEM((nz * chunk, nx * lanes), f32),
            pltpu.VMEM((EM_ITERS, nz * nx, chunk, lanes), f32),
            pltpu.VMEM((EM_ITERS, owners, chunk, lanes), f32),
            pltpu.SemaphoreType.DMA((STEPS, 5)),
            pltpu.SemaphoreType.DMA((STEPS, 5)),
        ]
        + [pltpu.SemaphoreType.DMA((EM_ITERS,))] * 6
        + [pltpu.SemaphoreType.DMA((7,))],
        compiler_params=pltpu.CompilerParams(
            collective_id=0, has_side_effects=True, vmem_limit_bytes=65400 * 1024
        ),
    )(image, brain_mask, labels, ana, syn, rowm, slabv)


def solution(mesh):
    placed = (
        P(None, ("grp", "slab"), "row", "col"),
        P(("grp", "slab"), "row", "col"),
        P(("grp", "slab"), "row", "col"),
    )
    return jax.shard_map(
        functools.partial(local, mesh.shape["slab"], mesh.shape["row"], mesh.shape["col"]),
        mesh=mesh,
        in_specs=placed,
        out_specs=(
            P(None, ("grp", "slab"), "row", "col"),
            P(None, ("grp", "slab"), "row", "col"),
            P("grp", None),
        ),
        check_vma=False,
    )
```

```python
import functools
import math

import jax
import jax.numpy as jnp
import numpy as np
from jax import lax
from jax.experimental import pallas as pl
from jax.experimental.pallas import tpu as pltpu
from jax.sharding import PartitionSpec as P

M = 3
K = 8
EM_ITERS = 2
MF_PASSES = 2
STEPS = EM_ITERS * MF_PASSES

MESH = pl.DeviceIdType.MESH
highest = lax.Precision.HIGHEST
coupling = 1.0
breadth = 8.0
f32 = jnp.float32


def response(length):
    folded = np.minimum(np.arange(length), length - np.arange(length)) / length
    return np.exp(-2.0 * np.pi**2 * (length / breadth) ** 2 * folded * folded)


def kernel_of(length):
    return np.real(np.fft.ifft(response(length)))


def column_tables(length):
    resp = response(length)
    kept = [j for j in range(length // 2 + 1) if np.float32(resp[j]) != 0]
    cells = np.arange(length)
    analysis, synthesis = [], []
    for j in kept:
        angle = 2.0 * np.pi * (j * cells % length) / length
        single = j == 0 or 2 * j == length
        weight = (1.0 if single else 2.0) * resp[j] / length
        analysis.append(np.cos(angle))
        synthesis.append(weight * np.cos(angle))
        if not single:
            analysis.append(np.sin(angle))
            synthesis.append(weight * np.sin(angle))
    rows = -(-len(analysis) // 8) * 8
    pad = np.zeros((rows - len(analysis), length))
    return np.concatenate([analysis, pad]), np.concatenate([synthesis, pad])


def row_matrix(nx, slabs, rows):
    line = kernel_of(nx * rows)
    at = np.arange(nx * rows)
    square = line[(at[None, :] - at[:, None]) % (nx * rows)].reshape(nx, rows, nx, rows)
    full = np.einsum("arbq,st->asrbtq", square, np.eye(slabs))
    size = nx * slabs * rows
    return full.reshape(size, size)


def slab_vectors(nz, slabs, rows):
    line = kernel_of(nz * slabs)
    out = np.zeros((nz, slabs, 1, slabs * rows))
    for dz in range(nz):
        for e in range(slabs):
            for s in range(slabs):
                value = line[(slabs * dz + s - (s - e) % slabs) % (nz * slabs)]
                out[dz, e, 0, s * rows : (s + 1) * rows] = value
    return out


def kernel(
    nz, nx, nc, chunk, owners,
    image_h, mask_h, labels_h, ana_h, syn_h, rowm_h, slabv_h,
    post, bias, means_out,
    image, mask, labels, ana, syn, rowm, slabv,
    bel, colh, cols, rowh, rows_s, corr, dens, res, mom, mom_s, mom_r, par,
    fwd_s, fwd_r, rolled, mixed, back_s, back_r,
    hs_sem, hr_sem, ms_sem, mr_sem, fs_sem, fr_sem, bs_sem, br_sem, in_sem,
):
    _, S, R, C = image.shape
    count = nz * nx * nc
    z, x, c = lax.axis_index("slab"), lax.axis_index("row"), lax.axis_index("col")
    me = (z * nx + x) * nc + c
    J = ana.shape[0]
    everyone = owners == count

    fetches = [
        pltpu.make_async_copy(src, dst, in_sem.at[n])
        for n, (src, dst) in enumerate(
            [
                (labels_h, labels), (mask_h, mask), (image_h, image), (ana_h.at[c], ana),
                (rowm_h, rowm), (slabv_h, slabv), (syn_h.at[c], syn),
            ]
        )
    ]
    for fetch in fetches:
        fetch.start()

    def moved(at, by, size):
        if size == 1:
            return at
        there = at + by
        return jnp.where(there >= size, there - size, there)

    def shifted(dz, dx, dc):
        zz, xx, cc = moved(z, dz, nz), moved(x, dx, nx), moved(c, dc, nc)
        return {"slab": zz, "row": xx, "col": cc}, (zz * nx + xx) * nc + cc

    def each(action):
        if count <= 32:
            for d in range(count - 1, 0, -1):
                action(*shifted(d // (nx * nc), d // nc % nx, d % nc))
        else:
            def body(d, carry):
                action(*shifted(d // (nx * nc), d // nc % nx, d % nc))
                return carry

            lax.fori_loop(1, count, body, 0)

    lane = lax.broadcasted_iota(jnp.int32, (R, C), 1)
    lane3 = lax.broadcasted_iota(jnp.int32, (K, R, C), 2)
    sub3 = lax.broadcasted_iota(jnp.int32, (K, R, C), 1)

    for v in range(STEPS):
        bel[v, :, 0] = jnp.zeros((K, R, C), f32)
        bel[v, :, S + 1] = jnp.zeros((K, R, C), f32)
    rowh[...] = jnp.zeros(rowh.shape, f32)

    barrier = pltpu.get_barrier_semaphore()

    each(
        lambda device, q: pl.semaphore_signal(
            barrier, inc=1, device_id=device, device_id_type=MESH
        )
    )

    def halo_copies(v):
        copies = [
            (z < nz - 1, z > 0, bel.at[v, :, S], bel.at[v, :, 0], {"slab": z + 1}, 0),
            (z > 0, z < nz - 1, bel.at[v, :, 1], bel.at[v, :, S + 1], {"slab": z - 1}, 1),
            (x < nx - 1, x > 0, rows_s.at[v, 1], rowh.at[v, 0], {"row": x + 1}, 2),
            (x > 0, x < nx - 1, rows_s.at[v, 0], rowh.at[v, 1], {"row": x - 1}, 3),
        ]
        if nc == 2:
            copies.append((None, None, cols.at[v], colh.at[v], {"col": 1 - c}, 4))
        out = []
        for sends, receives, src, dst, device, n in copies:
            copy = pltpu.make_async_remote_copy(
                src_ref=src, dst_ref=dst, send_sem=hs_sem.at[v, n], recv_sem=hr_sem.at[v, n],
                device_id=device, device_id_type=MESH,
            )
            out.append((sends, receives, copy))
        return out

    def under(condition, action):
        if condition is None:
            action()
        else:
            pl.when(condition)(action)

    def halo_start(v, first=0, last=5):
        for sends, _, copy in halo_copies(v)[first:last]:
            under(sends, copy.start)

    def halo_wait(v):
        for _, receives, copy in halo_copies(v):
            under(receives, copy.wait_recv)

    def halo_drain(v):
        for sends, _, copy in halo_copies(v):
            under(sends, copy.wait_send)

    def keep(v, s, block):
        bel[v, :, s + 1] = block
        rows_s[v, 0, s] = block[:, 0]
        rows_s[v, 1, s] = block[:, R - 1]
        if nc == 2:
            packed = jnp.zeros((R, C), f32)
            for k in range(K):
                last = jnp.broadcast_to(block[k, :, C - 1 : C], (R, C))
                first = jnp.broadcast_to(block[k, :, 0:1], (R, C))
                packed = jnp.where(lane == k, jnp.where(c == 0, last, first), packed)
            cols[v, s] = packed

    def begin(s, carry):
        seen = labels[s]
        inside = mask[s].astype(f32)
        block = jnp.stack([jnp.where(seen == k, inside, 0.0) for k in range(K)])
        keep(0, s, block)
        return carry

    fetches[0].wait()
    fetches[1].wait()
    lax.fori_loop(0, S, begin, 0, unroll=True)
    mom[...] = jnp.zeros(mom.shape, f32)
    fetches[2].wait()

    def send(src, dst, send_sem, recv_sem, device):
        pltpu.make_async_remote_copy(
            src_ref=src, dst_ref=dst, send_sem=send_sem, recv_sem=recv_sem,
            device_id=device, device_id_type=MESH,
        ).start()

    def await_bytes(buffer, n, sem):
        whole = buffer.at[pl.ds(0, n)]
        pltpu.make_async_copy(whole, whole, sem).wait()

    def moments_out(it):
        for k in range(K):
            weight = bel[it * MF_PASSES, k, 1 : S + 1]
            total = jnp.sum(jnp.sum(weight, axis=0), axis=0, keepdims=True)
            for m in range(M):
                value = corr[m] if it else image[m]
                first = weight * value
                second = first * value
                mom[m * K + k : m * K + k + 1] = total
                at = (M + m) * K + k
                mom[at : at + 1] = jnp.sum(jnp.sum(first, axis=0), axis=0, keepdims=True)
                at = (2 * M + m) * K + k
                mom[at : at + 1] = jnp.sum(jnp.sum(second, axis=0), axis=0, keepdims=True)
        sums = lax.dot_general(
            jnp.ones((8, C), f32), mom[...], (((1,), (1,)), ((), ())),
            precision=highest, preferred_element_type=f32,
        )
        mom_s[it] = sums[0:1]
        if it == 0:
            pl.semaphore_wait(barrier, count - 1)
        each(
            lambda device, q: send(
                mom_s.at[it], mom_r.at[it, me], ms_sem.at[it], mr_sem.at[it], device
            )
        )
        halo_start(it * MF_PASSES)
        mom_r[it, me] = sums[0:1]

    def moments_in(it):
        await_bytes(mom_r.at[it], count - 1, mr_sem.at[it])
        sums = jnp.broadcast_to(jnp.sum(mom_r[it], axis=0), (8, 128))
        width = M * K
        lanes = lax.broadcasted_iota(jnp.int32, (8, 128), 1)
        counts = sums
        first = pltpu.roll(sums, 128 - width, 1)
        second = pltpu.roll(sums, 128 - 2 * width, 1)
        scale = 1.0 / (counts + 1.0)
        means = first * scale
        spread = second - 2.0 * means * first + means * means * counts
        variance = jnp.where(lanes < width, (spread + 1.0) * scale, 1.0)
        half = 0.5 / variance
        logs = jnp.log(variance)
        everything = jnp.sum(jnp.where(lanes < K, counts, 0.0), axis=1, keepdims=True)
        prior = jnp.where(lanes < K, (counts + 1.0) / (everything + K), 1.0)
        logs_sum = logs
        for m in range(1, M):
            logs_sum = logs_sum + pltpu.roll(logs, 128 - m * K, 1)
        base = jnp.log(prior) - 0.5 * logs_sum
        for n in range(width):
            par[n] = jnp.broadcast_to(means[:, n : n + 1], (8, 128))
            par[width + n] = jnp.broadcast_to(half[:, n : n + 1], (8, 128))
        for k in range(K):
            par[2 * width + k] = jnp.broadcast_to(base[:, k : k + 1], (8, 128))
        if it == EM_ITERS - 1:
            rows = lax.broadcasted_iota(jnp.int32, (8, 128), 0)
            table = jnp.zeros((8, 128), f32)
            for k in range(K):
                for m in range(M):
                    table = jnp.where((rows == k) & (lanes == m), par[m * K + k], table)
            means_out[...] = table[:K, :M]

    def param(n):
        one = par[n, 0:1]
        return jnp.broadcast_to(one, (R, C))

    def residual(it):
        v = it * MF_PASSES

        def body(s, carry):
            block = bel[v, :, s + 1]
            total = jnp.sum(block, axis=0)
            for m in range(M):
                value = image[m, s] * total
                for k in range(K):
                    value = value - block[k] * param(m * K + k)
                res[m, s] = value
            return carry

        lax.fori_loop(0, S, body, 0, unroll=True)

    def smooth(it):
        if it == 0:
            fetches[3].wait()
        table = ana[...]
        coefs = [
            lax.dot_general(
                table, res[m].reshape(S * R, C), (((1,), (1,)), ((), ())),
                precision=highest, preferred_element_type=f32,
            )
            for m in range(M)
        ]
        tall = jnp.concatenate(coefs, axis=0)
        spare = owners * chunk - M * J
        if spare:
            tall = jnp.concatenate([tall, jnp.zeros((spare, S * R), f32)], axis=0)
        fwd_s[it] = tall.reshape(owners, chunk, S * R)

        def forward(device, q):
            def go():
                send(fwd_s.at[it, q], fwd_r.at[it, me], fs_sem.at[it], fr_sem.at[it], device)

            under(None if everyone else q < owners, go)

        each(forward)
        if it == 0:
            fetches[4].wait()
            fetches[5].wait()

        def own():
            fwd_r[it, me] = fwd_s[it, me]
            await_bytes(fwd_r.at[it], count - 1, fr_sem.at[it])
            stack = []
            for zz in range(nz):
                across = []
                for xx in range(nx):
                    at = (zz * nx + xx) * nc
                    tile = fwd_r[it, at]
                    for cc in range(1, nc):
                        tile = tile + fwd_r[it, at + cc]
                    across.append(tile)
                stack.append(jnp.concatenate(across, axis=1))
            mixed[...] = jnp.dot(
                jnp.concatenate(stack, axis=0), rowm[...],
                precision=highest, preferred_element_type=f32,
            )
            for xx in range(nx):
                for zz in range(nz):
                    tile = mixed[zz * chunk : (zz + 1) * chunk, xx * S * R : (xx + 1) * S * R]
                    for e in range(S):
                        rolled[zz, e] = pltpu.roll(tile, e * R, 1) if e else tile

                def body(zq, carry):
                    total = jnp.zeros((chunk, S * R), f32)
                    for zz in range(nz):
                        dz = lax.rem(zq + nz - zz, nz)
                        for e in range(S):
                            total = total + rolled[zz, e] * slabv[dz, e]
                    back_s[it, zq * nx + xx] = total
                    return carry

                lax.fori_loop(0, nz, body, 0, unroll=nz <= 4)
            each(
                lambda device, q: send(
                    back_s.at[it, q // nc], back_r.at[it, me], bs_sem.at[it], br_sem.at[it], device
                )
            )
            back_r[it, me] = back_s[it, me // nc]

        under(None if everyone else me < owners, own)
        if it == 0:
            fetches[6].wait()
        if everyone:
            await_bytes(back_r.at[it], owners - 1, br_sem.at[it])
        else:
            under(me < owners, lambda: await_bytes(back_r.at[it], owners - 1, br_sem.at[it]))
            under(me >= owners, lambda: await_bytes(back_r.at[it], owners, br_sem.at[it]))
        flat = back_r[it].reshape(owners * chunk, S * R)
        table = syn[...]
        for m in range(M):
            field = lax.dot_general(
                flat[m * J : (m + 1) * J], table, (((0,), (0,)), ((), ())),
                precision=highest, preferred_element_type=f32,
            ).reshape(S, R, C)
            if it == EM_ITERS - 1:
                bias[m] = field
            corr[m] = image[m] - field

    def density():
        width = M * K

        def body(s, carry):
            for k in range(K):
                value = param(2 * width + k)
                for m in range(M):
                    offset = corr[m, s] - param(m * K + k)
                    value = value - offset * offset * param(width + m * K + k)
                dens[k, s] = value
            return carry

        lax.fori_loop(0, S, body, 0, unroll=True)

    def sweep(v):
        edge = jnp.where(c == 0, C - 1, 0)

        def body(s, carry):
            block = bel[v, :, s + 1]
            total = bel[v, :, s] + bel[v, :, s + 2]
            total = total + jnp.where(sub3 == 0, rowh[v, 0, s][:, None, :], pltpu.roll(block, 1, 1))
            total = total + jnp.where(
                sub3 == R - 1, rowh[v, 1, s][:, None, :], pltpu.roll(block, R - 1, 1)
            )
            if nc == 2:
                packed = colh[v, s]
                beyond = jnp.stack(
                    [jnp.broadcast_to(packed[:, k : k + 1], (R, C)) for k in range(K)]
                )
                total = total + jnp.where(lane3 == edge, beyond, 0.0)
            total = total + jnp.where(lane3 == 0, 0.0, pltpu.roll(block, 1, 2))
            total = total + jnp.where(lane3 == C - 1, 0.0, pltpu.roll(block, C - 1, 2))
            logits = dens[:, s] + coupling * total
            powers = jnp.exp(logits - jnp.max(logits, axis=0, keepdims=True))
            scale = mask[s].astype(f32) / jnp.sum(powers, axis=0)
            fresh = powers * scale[None]
            if v == STEPS - 1:
                post[:, s] = fresh.astype(post.dtype)
            else:
                keep(v + 1, s, fresh)
            return carry

        body(0, 0)
        body(S - 1, 0)
        if v % MF_PASSES < MF_PASSES - 1:
            halo_start(v + 1, 0, 2)
        lax.fori_loop(1, S - 1, body, 0, unroll=True)
        if v % MF_PASSES < MF_PASSES - 1:
            halo_start(v + 1, 2, 5)

    for it in range(EM_ITERS):
        moments_out(it)
        moments_in(it)
        residual(it)
        smooth(it)
        density()
        for p in range(MF_PASSES):
            v = it * MF_PASSES + p
            halo_wait(v)
            sweep(v)

    for v in range(STEPS):
        halo_drain(v)
    for it in range(EM_ITERS):
        await_bytes(mom_r.at[it], count - 1, ms_sem.at[it])
        if everyone:
            await_bytes(fwd_r.at[it], owners - 1, fs_sem.at[it])
            await_bytes(fwd_r.at[it], count - 1, bs_sem.at[it])
        else:
            under(me >= owners, lambda: await_bytes(fwd_r.at[it], owners, fs_sem.at[it]))

            def drain():
                if owners > 1:
                    await_bytes(fwd_r.at[it], owners - 1, fs_sem.at[it])
                await_bytes(fwd_r.at[it], count - 1, bs_sem.at[it])

            under(me < owners, drain)


def local(nz, nx, nc, image, brain_mask, labels):
    _, S, R, C = image.shape
    count = nz * nx * nc
    analysis, synthesis = column_tables(C * nc)
    J = analysis.shape[0]
    tiles = M * J // 8
    chunk = 8 * -(-tiles // count)
    owners = -(-M * J // chunk)
    if count <= 2 * owners:
        owners = count
    ana = jnp.asarray(analysis.reshape(J, nc, C).transpose(1, 0, 2), f32)
    syn = jnp.asarray(synthesis.reshape(J, nc, C).transpose(1, 0, 2), f32)
    rowm = jnp.asarray(row_matrix(nx, S, R), f32)
    slabv = jnp.asarray(slab_vectors(nz, S, R), f32)
    vmem = pl.BlockSpec(memory_space=pltpu.VMEM)
    lanes = S * R
    return pl.pallas_call(
        functools.partial(kernel, nz, nx, nc, chunk, owners),
        out_shape=(
            jax.ShapeDtypeStruct((K, S, R, C), jnp.bfloat16),
            jax.ShapeDtypeStruct((M, S, R, C), f32),
            jax.ShapeDtypeStruct((K, M), f32),
        ),
        in_specs=[pl.BlockSpec(memory_space=pl.ANY)] * 7,
        out_specs=(vmem, vmem, vmem),
        scratch_shapes=[
            pltpu.VMEM((M, S, R, C), f32),
            pltpu.VMEM((S, R, C), jnp.int32),
            pltpu.VMEM((S, R, C), jnp.int32),
            pltpu.VMEM((J, C), f32),
            pltpu.VMEM((J, C), f32),
            pltpu.VMEM(rowm.shape, f32),
            pltpu.VMEM(slabv.shape, f32),
            pltpu.VMEM((STEPS, K, S + 2, R, C), f32),
            pltpu.VMEM((STEPS, S, R, C), f32),
            pltpu.VMEM((STEPS, S, R, C), f32),
            pltpu.VMEM((STEPS, 2, S, K, C), f32),
            pltpu.VMEM((STEPS, 2, S, K, C), f32),
            pltpu.VMEM((M, S, R, C), f32),
            pltpu.VMEM((K, S, R, C), f32),
            pltpu.VMEM((M, S, R, C), f32),
            pltpu.VMEM((128, C), f32),
            pltpu.VMEM((EM_ITERS, 1, 128), f32),
            pltpu.VMEM((EM_ITERS, count, 1, 128), f32),
            pltpu.VMEM((2 * M * K + K, 8, 128), f32),
            pltpu.VMEM((EM_ITERS, owners, chunk, lanes), f32),
            pltpu.VMEM((EM_ITERS, count, chunk, lanes), f32),
            pltpu.VMEM((nz, S, chunk, lanes), f32),
            pltpu.VMEM((nz * chunk, nx * lanes), f32),
            pltpu.VMEM((EM_ITERS, nz * nx, chunk, lanes), f32),
            pltpu.VMEM((EM_ITERS, owners, chunk, lanes), f32),
            pltpu.SemaphoreType.DMA((STEPS, 5)),
            pltpu.SemaphoreType.DMA((STEPS, 5)),
        ]
        + [pltpu.SemaphoreType.DMA((EM_ITERS,))] * 6
        + [pltpu.SemaphoreType.DMA((7,))],
        compiler_params=pltpu.CompilerParams(
            collective_id=0, has_side_effects=True, vmem_limit_bytes=65400 * 1024
        ),
    )(image, brain_mask, labels, ana, syn, rowm, slabv)


def solution(mesh):
    placed = (
        P(None, ("grp", "slab"), "row", "col"),
        P(("grp", "slab"), "row", "col"),
        P(("grp", "slab"), "row", "col"),
    )
    return jax.shard_map(
        functools.partial(local, mesh.shape["slab"], mesh.shape["row"], mesh.shape["col"]),
        mesh=mesh,
        in_specs=placed,
        out_specs=(
            P(None, ("grp", "slab"), "row", "col"),
            P(None, ("grp", "slab"), "row", "col"),
            P("grp", None),
        ),
        check_vma=False,
    )
```

```python
import functools
import math

import jax
import jax.numpy as jnp
import numpy as np
from jax import lax
from jax.experimental import pallas as pl
from jax.experimental.pallas import tpu as pltpu
from jax.sharding import PartitionSpec as P

M = 3
K = 8
EM_ITERS = 2
MF_PASSES = 2
STEPS = EM_ITERS * MF_PASSES

MESH = pl.DeviceIdType.MESH
highest = lax.Precision.HIGHEST
coupling = 1.0
breadth = 8.0
f32 = jnp.float32


def response(length):
    folded = np.minimum(np.arange(length), length - np.arange(length)) / length
    return np.exp(-2.0 * np.pi**2 * (length / breadth) ** 2 * folded * folded)


def kernel_of(length):
    return np.real(np.fft.ifft(response(length)))


def column_tables(length):
    resp = response(length)
    kept = [j for j in range(length // 2 + 1) if np.float32(resp[j]) != 0]
    cells = np.arange(length)
    analysis, synthesis = [], []
    for j in kept:
        angle = 2.0 * np.pi * (j * cells % length) / length
        single = j == 0 or 2 * j == length
        weight = (1.0 if single else 2.0) * resp[j] / length
        analysis.append(np.cos(angle))
        synthesis.append(weight * np.cos(angle))
        if not single:
            analysis.append(np.sin(angle))
            synthesis.append(weight * np.sin(angle))
    rows = -(-len(analysis) // 8) * 8
    pad = np.zeros((rows - len(analysis), length))
    return np.concatenate([analysis, pad]), np.concatenate([synthesis, pad])


def row_matrix(nx, slabs, rows):
    line = kernel_of(nx * rows)
    at = np.arange(nx * rows)
    square = line[(at[None, :] - at[:, None]) % (nx * rows)].reshape(nx, rows, nx, rows)
    full = np.einsum("arbq,st->asrbtq", square, np.eye(slabs))
    size = nx * slabs * rows
    return full.reshape(size, size)


def slab_vectors(nz, slabs, rows):
    line = kernel_of(nz * slabs)
    out = np.zeros((nz, slabs, 1, slabs * rows))
    for dz in range(nz):
        for e in range(slabs):
            for s in range(slabs):
                value = line[(slabs * dz + s - (s - e) % slabs) % (nz * slabs)]
                out[dz, e, 0, s * rows : (s + 1) * rows] = value
    return out


def kernel(
    nz, nx, nc, chunk, owners,
    image_h, mask_h, labels_h, ana_h, syn_h, rowm_h, slabv_h,
    post, bias, means_out,
    image, mask, labels, ana, syn, rowm, slabv,
    bel, colh, cols, rowh, rows_s, corr, dens, res, mom, mom_s, mom_r, par,
    fwd_s, fwd_r, rolled, mixed, back_s, back_r,
    hs_sem, hr_sem, ms_sem, mr_sem, fs_sem, fr_sem, bs_sem, br_sem, in_sem,
):
    _, S, R, C = image.shape
    count = nz * nx * nc
    z, x, c = lax.axis_index("slab"), lax.axis_index("row"), lax.axis_index("col")
    me = (z * nx + x) * nc + c
    J = ana.shape[0]
    everyone = owners == count

    fetches = [
        pltpu.make_async_copy(src, dst, in_sem.at[n])
        for n, (src, dst) in enumerate(
            [
                (labels_h, labels), (mask_h, mask), (image_h, image), (ana_h.at[c], ana),
                (rowm_h, rowm), (slabv_h, slabv), (syn_h.at[c], syn),
            ]
        )
    ]
    for fetch in fetches:
        fetch.start()

    def moved(at, by, size):
        if size == 1:
            return at
        there = at + by
        return jnp.where(there >= size, there - size, there)

    def shifted(dz, dx, dc):
        zz, xx, cc = moved(z, dz, nz), moved(x, dx, nx), moved(c, dc, nc)
        return {"slab": zz, "row": xx, "col": cc}, (zz * nx + xx) * nc + cc

    def each(action):
        if count <= 32:
            for d in range(count - 1, 0, -1):
                action(*shifted(d // (nx * nc), d // nc % nx, d % nc))
        else:
            def body(d, carry):
                action(*shifted(d // (nx * nc), d // nc % nx, d % nc))
                return carry

            lax.fori_loop(1, count, body, 0)

    lane = lax.broadcasted_iota(jnp.int32, (R, C), 1)
    lane3 = lax.broadcasted_iota(jnp.int32, (K, R, C), 2)
    sub3 = lax.broadcasted_iota(jnp.int32, (K, R, C), 1)

    for v in range(STEPS):
        bel[v, :, 0] = jnp.zeros((K, R, C), f32)
        bel[v, :, S + 1] = jnp.zeros((K, R, C), f32)
    rowh[...] = jnp.zeros(rowh.shape, f32)

    barrier = pltpu.get_barrier_semaphore()

    each(
        lambda device, q: pl.semaphore_signal(
            barrier, inc=1, device_id=device, device_id_type=MESH
        )
    )

    def halo_copies(v):
        copies = [
            (z < nz - 1, z > 0, bel.at[v, :, S], bel.at[v, :, 0], {"slab": z + 1}, 0),
            (z > 0, z < nz - 1, bel.at[v, :, 1], bel.at[v, :, S + 1], {"slab": z - 1}, 1),
            (x < nx - 1, x > 0, rows_s.at[v, 1], rowh.at[v, 0], {"row": x + 1}, 2),
            (x > 0, x < nx - 1, rows_s.at[v, 0], rowh.at[v, 1], {"row": x - 1}, 3),
        ]
        if nc == 2:
            copies.append((None, None, cols.at[v], colh.at[v], {"col": 1 - c}, 4))
        out = []
        for sends, receives, src, dst, device, n in copies:
            copy = pltpu.make_async_remote_copy(
                src_ref=src, dst_ref=dst, send_sem=hs_sem.at[v, n], recv_sem=hr_sem.at[v, n],
                device_id=device, device_id_type=MESH,
            )
            out.append((sends, receives, copy))
        return out

    def under(condition, action):
        if condition is None:
            action()
        else:
            pl.when(condition)(action)

    def halo_start(v, first=0, last=5):
        for sends, _, copy in halo_copies(v)[first:last]:
            under(sends, copy.start)

    def halo_wait(v):
        for _, receives, copy in halo_copies(v):
            under(receives, copy.wait_recv)

    def halo_drain(v):
        for sends, _, copy in halo_copies(v):
            under(sends, copy.wait_send)

    def keep(v, s, block):
        bel[v, :, s + 1] = block
        rows_s[v, 0, s] = block[:, 0]
        rows_s[v, 1, s] = block[:, R - 1]
        if nc == 2:
            packed = jnp.zeros((R, C), f32)
            for k in range(K):
                last = jnp.broadcast_to(block[k, :, C - 1 : C], (R, C))
                first = jnp.broadcast_to(block[k, :, 0:1], (R, C))
                packed = jnp.where(lane == k, jnp.where(c == 0, last, first), packed)
            cols[v, s] = packed

    def begin(s, carry):
        seen = labels[s]
        inside = mask[s].astype(f32)
        block = jnp.stack([jnp.where(seen == k, inside, 0.0) for k in range(K)])
        keep(0, s, block)
        return carry

    fetches[0].wait()
    fetches[1].wait()
    lax.fori_loop(0, S, begin, 0, unroll=True)
    mom[...] = jnp.zeros(mom.shape, f32)
    fetches[2].wait()

    def send(src, dst, send_sem, recv_sem, device):
        pltpu.make_async_remote_copy(
            src_ref=src, dst_ref=dst, send_sem=send_sem, recv_sem=recv_sem,
            device_id=device, device_id_type=MESH,
        ).start()

    def await_bytes(buffer, n, sem):
        whole = buffer.at[pl.ds(0, n)]
        pltpu.make_async_copy(whole, whole, sem).wait()

    def moments_out(it):
        for k in range(K):
            weight = bel[it * MF_PASSES, k, 1 : S + 1]
            total = jnp.sum(jnp.sum(weight, axis=0), axis=0, keepdims=True)
            for m in range(M):
                value = corr[m] if it else image[m]
                first = weight * value
                second = first * value
                mom[m * K + k : m * K + k + 1] = total
                at = (M + m) * K + k
                mom[at : at + 1] = jnp.sum(jnp.sum(first, axis=0), axis=0, keepdims=True)
                at = (2 * M + m) * K + k
                mom[at : at + 1] = jnp.sum(jnp.sum(second, axis=0), axis=0, keepdims=True)
        sums = lax.dot_general(
            jnp.ones((8, C), f32), mom[...], (((1,), (1,)), ((), ())),
            precision=highest, preferred_element_type=f32,
        )
        mom_s[it] = sums[0:1]
        if it == 0:
            pl.semaphore_wait(barrier, count - 1)
        each(
            lambda device, q: send(
                mom_s.at[it], mom_r.at[it, me], ms_sem.at[it], mr_sem.at[it], device
            )
        )
        halo_start(it * MF_PASSES)
        mom_r[it, me] = sums[0:1]

    def moments_in(it):
        await_bytes(mom_r.at[it], count - 1, mr_sem.at[it])
        sums = jnp.broadcast_to(jnp.sum(mom_r[it], axis=0), (8, 128))
        width = M * K
        lanes = lax.broadcasted_iota(jnp.int32, (8, 128), 1)
        counts = sums
        first = pltpu.roll(sums, 128 - width, 1)
        second = pltpu.roll(sums, 128 - 2 * width, 1)
        scale = 1.0 / (counts + 1.0)
        means = first * scale
        spread = second - 2.0 * means * first + means * means * counts
        variance = jnp.where(lanes < width, (spread + 1.0) * scale, 1.0)
        half = 0.5 / variance
        logs = jnp.log(variance)
        everything = jnp.sum(jnp.where(lanes < K, counts, 0.0), axis=1, keepdims=True)
        prior = jnp.where(lanes < K, (counts + 1.0) / (everything + K), 1.0)
        logs_sum = logs
        for m in range(1, M):
            logs_sum = logs_sum + pltpu.roll(logs, 128 - m * K, 1)
        base = jnp.log(prior) - 0.5 * logs_sum
        for n in range(width):
            par[n] = jnp.broadcast_to(means[:, n : n + 1], (8, 128))
            par[width + n] = jnp.broadcast_to(half[:, n : n + 1], (8, 128))
        for k in range(K):
            par[2 * width + k] = jnp.broadcast_to(base[:, k : k + 1], (8, 128))
        if it == EM_ITERS - 1:
            rows = lax.broadcasted_iota(jnp.int32, (8, 128), 0)
            table = jnp.zeros((8, 128), f32)
            for k in range(K):
                for m in range(M):
                    table = jnp.where((rows == m) & (lanes == k), par[m * K + k], table)
            means_out[...] = table[:M, :K]

    def param(n):
        one = par[n, 0:1]
        return jnp.broadcast_to(one, (R, C))

    def residual(it):
        v = it * MF_PASSES

        def body(s, carry):
            block = bel[v, :, s + 1]
            total = jnp.sum(block, axis=0)
            for m in range(M):
                value = image[m, s] * total
                for k in range(K):
                    value = value - block[k] * param(m * K + k)
                res[m, s] = value
            return carry

        lax.fori_loop(0, S, body, 0, unroll=True)

    def smooth(it):
        if it == 0:
            fetches[3].wait()
        table = ana[...]
        coefs = [
            lax.dot_general(
                table, res[m].reshape(S * R, C), (((1,), (1,)), ((), ())),
                precision=highest, preferred_element_type=f32,
            )
            for m in range(M)
        ]
        tall = jnp.concatenate(coefs, axis=0)
        spare = owners * chunk - M * J
        if spare:
            tall = jnp.concatenate([tall, jnp.zeros((spare, S * R), f32)], axis=0)
        fwd_s[it] = tall.reshape(owners, chunk, S * R)

        def forward(device, q):
            def go():
                send(fwd_s.at[it, q], fwd_r.at[it, me], fs_sem.at[it], fr_sem.at[it], device)

            under(None if everyone else q < owners, go)

        each(forward)
        if it == 0:
            fetches[4].wait()
            fetches[5].wait()

        def own():
            fwd_r[it, me] = fwd_s[it, me]
            await_bytes(fwd_r.at[it], count - 1, fr_sem.at[it])
            stack = []
            for zz in range(nz):
                across = []
                for xx in range(nx):
                    at = (zz * nx + xx) * nc
                    tile = fwd_r[it, at]
                    for cc in range(1, nc):
                        tile = tile + fwd_r[it, at + cc]
                    across.append(tile)
                stack.append(jnp.concatenate(across, axis=1))
            mixed[...] = jnp.dot(
                jnp.concatenate(stack, axis=0), rowm[...],
                precision=highest, preferred_element_type=f32,
            )
            for xx in range(nx):
                for zz in range(nz):
                    tile = mixed[zz * chunk : (zz + 1) * chunk, xx * S * R : (xx + 1) * S * R]
                    for e in range(S):
                        rolled[zz, e] = pltpu.roll(tile, e * R, 1) if e else tile

                def body(zq, carry):
                    total = jnp.zeros((chunk, S * R), f32)
                    for zz in range(nz):
                        dz = lax.rem(zq + nz - zz, nz)
                        for e in range(S):
                            total = total + rolled[zz, e] * slabv[dz, e]
                    back_s[it, zq * nx + xx] = total
                    return carry

                lax.fori_loop(0, nz, body, 0, unroll=nz <= 4)
            each(
                lambda device, q: send(
                    back_s.at[it, q // nc], back_r.at[it, me], bs_sem.at[it], br_sem.at[it], device
                )
            )
            back_r[it, me] = back_s[it, me // nc]

        under(None if everyone else me < owners, own)
        if it == 0:
            fetches[6].wait()
        if everyone:
            await_bytes(back_r.at[it], owners - 1, br_sem.at[it])
        else:
            under(me < owners, lambda: await_bytes(back_r.at[it], owners - 1, br_sem.at[it]))
            under(me >= owners, lambda: await_bytes(back_r.at[it], owners, br_sem.at[it]))
        flat = back_r[it].reshape(owners * chunk, S * R)
        table = syn[...]
        for m in range(M):
            field = lax.dot_general(
                flat[m * J : (m + 1) * J], table, (((0,), (0,)), ((), ())),
                precision=highest, preferred_element_type=f32,
            ).reshape(S, R, C)
            if it == EM_ITERS - 1:
                bias[m] = field
            corr[m] = image[m] - field

    def density():
        width = M * K

        def body(s, carry):
            for k in range(K):
                value = param(2 * width + k)
                for m in range(M):
                    offset = corr[m, s] - param(m * K + k)
                    value = value - offset * offset * param(width + m * K + k)
                dens[k, s] = value
            return carry

        lax.fori_loop(0, S, body, 0, unroll=True)

    def sweep(v):
        edge = jnp.where(c == 0, C - 1, 0)

        def body(s, carry):
            block = bel[v, :, s + 1]
            total = bel[v, :, s] + bel[v, :, s + 2]
            total = total + jnp.where(sub3 == 0, rowh[v, 0, s][:, None, :], pltpu.roll(block, 1, 1))
            total = total + jnp.where(
                sub3 == R - 1, rowh[v, 1, s][:, None, :], pltpu.roll(block, R - 1, 1)
            )
            if nc == 2:
                packed = colh[v, s]
                beyond = jnp.stack(
                    [jnp.broadcast_to(packed[:, k : k + 1], (R, C)) for k in range(K)]
                )
                total = total + jnp.where(lane3 == edge, beyond, 0.0)
            total = total + jnp.where(lane3 == 0, 0.0, pltpu.roll(block, 1, 2))
            total = total + jnp.where(lane3 == C - 1, 0.0, pltpu.roll(block, C - 1, 2))
            logits = dens[:, s] + coupling * total
            powers = jnp.exp(logits - jnp.max(logits, axis=0, keepdims=True))
            scale = mask[s].astype(f32) / jnp.sum(powers, axis=0)
            fresh = powers * scale[None]
            if v == STEPS - 1:
                post[:, s] = fresh.astype(post.dtype)
            else:
                keep(v + 1, s, fresh)
            return carry

        body(0, 0)
        body(S - 1, 0)
        if v % MF_PASSES < MF_PASSES - 1:
            halo_start(v + 1, 0, 2)
        lax.fori_loop(1, S - 1, body, 0, unroll=True)
        if v % MF_PASSES < MF_PASSES - 1:
            halo_start(v + 1, 2, 5)

    for it in range(EM_ITERS):
        moments_out(it)
        moments_in(it)
        residual(it)
        smooth(it)
        density()
        for p in range(MF_PASSES):
            v = it * MF_PASSES + p
            halo_wait(v)
            sweep(v)

    for v in range(STEPS):
        halo_drain(v)
    for it in range(EM_ITERS):
        await_bytes(mom_r.at[it], count - 1, ms_sem.at[it])
        if everyone:
            await_bytes(fwd_r.at[it], owners - 1, fs_sem.at[it])
            await_bytes(fwd_r.at[it], count - 1, bs_sem.at[it])
        else:
            under(me >= owners, lambda: await_bytes(fwd_r.at[it], owners, fs_sem.at[it]))

            def drain():
                if owners > 1:
                    await_bytes(fwd_r.at[it], owners - 1, fs_sem.at[it])
                await_bytes(fwd_r.at[it], count - 1, bs_sem.at[it])

            under(me < owners, drain)


def local(nz, nx, nc, image, brain_mask, labels):
    _, S, R, C = image.shape
    count = nz * nx * nc
    analysis, synthesis = column_tables(C * nc)
    J = analysis.shape[0]
    tiles = M * J // 8
    chunk = 8 * -(-tiles // count)
    owners = -(-M * J // chunk)
    if count <= 2 * owners:
        owners = count
    ana = jnp.asarray(analysis.reshape(J, nc, C).transpose(1, 0, 2), f32)
    syn = jnp.asarray(synthesis.reshape(J, nc, C).transpose(1, 0, 2), f32)
    rowm = jnp.asarray(row_matrix(nx, S, R), f32)
    slabv = jnp.asarray(slab_vectors(nz, S, R), f32)
    vmem = pl.BlockSpec(memory_space=pltpu.VMEM)
    lanes = S * R
    posterior, bias_field, means = pl.pallas_call(
        functools.partial(kernel, nz, nx, nc, chunk, owners),
        out_shape=(
            jax.ShapeDtypeStruct((K, S, R, C), jnp.bfloat16),
            jax.ShapeDtypeStruct((M, S, R, C), f32),
            jax.ShapeDtypeStruct((M, K), f32),
        ),
        in_specs=[pl.BlockSpec(memory_space=pl.ANY)] * 7,
        out_specs=(vmem, vmem, vmem),
        scratch_shapes=[
            pltpu.VMEM((M, S, R, C), f32),
            pltpu.VMEM((S, R, C), jnp.int32),
            pltpu.VMEM((S, R, C), jnp.int32),
            pltpu.VMEM((J, C), f32),
            pltpu.VMEM((J, C), f32),
            pltpu.VMEM(rowm.shape, f32),
            pltpu.VMEM(slabv.shape, f32),
            pltpu.VMEM((STEPS, K, S + 2, R, C), f32),
            pltpu.VMEM((STEPS, S, R, C), f32),
            pltpu.VMEM((STEPS, S, R, C), f32),
            pltpu.VMEM((STEPS, 2, S, K, C), f32),
            pltpu.VMEM((STEPS, 2, S, K, C), f32),
            pltpu.VMEM((M, S, R, C), f32),
            pltpu.VMEM((K, S, R, C), f32),
            pltpu.VMEM((M, S, R, C), f32),
            pltpu.VMEM((128, C), f32),
            pltpu.VMEM((EM_ITERS, 1, 128), f32),
            pltpu.VMEM((EM_ITERS, count, 1, 128), f32),
            pltpu.VMEM((2 * M * K + K, 8, 128), f32),
            pltpu.VMEM((EM_ITERS, owners, chunk, lanes), f32),
            pltpu.VMEM((EM_ITERS, count, chunk, lanes), f32),
            pltpu.VMEM((nz, S, chunk, lanes), f32),
            pltpu.VMEM((nz * chunk, nx * lanes), f32),
            pltpu.VMEM((EM_ITERS, nz * nx, chunk, lanes), f32),
            pltpu.VMEM((EM_ITERS, owners, chunk, lanes), f32),
            pltpu.SemaphoreType.DMA((STEPS, 5)),
            pltpu.SemaphoreType.DMA((STEPS, 5)),
        ]
        + [pltpu.SemaphoreType.DMA((EM_ITERS,))] * 6
        + [pltpu.SemaphoreType.DMA((7,))],
        compiler_params=pltpu.CompilerParams(
            collective_id=0, has_side_effects=True, vmem_limit_bytes=65400 * 1024
        ),
    )(image, brain_mask, labels, ana, syn, rowm, slabv)
    return posterior, bias_field, means.T


def solution(mesh):
    placed = (
        P(None, ("grp", "slab"), "row", "col"),
        P(("grp", "slab"), "row", "col"),
        P(("grp", "slab"), "row", "col"),
    )
    return jax.shard_map(
        functools.partial(local, mesh.shape["slab"], mesh.shape["row"], mesh.shape["col"]),
        mesh=mesh,
        in_specs=placed,
        out_specs=(
            P(None, ("grp", "slab"), "row", "col"),
            P(None, ("grp", "slab"), "row", "col"),
            P("grp", None),
        ),
        check_vma=False,
    )
```
